256 devices in a mesh: rep: 4 (over z_lo), fsdp: 64 (over x, z_hi, y, core).
Axes of the slice: x: 4, y: 4, z: 8 (z_hi: 2, z_lo: 4; z = z_hi * 4 + z_lo), core: 2. Of those that a mesh axis runs over, the one named last changes fastest.
Arguments:
- acts: bfloat16 [196608, 8192], P(('rep', 'fsdp')), may hold values from -24 to 24
- cotangent: bfloat16 [196608, 512], P(('rep', 'fsdp')), may hold values from -0.02734375 to 0.02734375
- momentum: float32 [4, 8192, 512], P('rep', 'fsdp'), may hold values from -6 to 6
- params: float32 [8192, 512], P('fsdp'), may hold values from -0.6 to 0.6
- band_index: int32 [128, 8, 128], P('fsdp'), may hold values from 0 to 2015, as said below
Outputs:
- new_momentum: float32 [4, 8192, 512], P('rep', 'fsdp')
- new_params: float32 [8192, 512], P('fsdp')
The draws below stay inside these ranges and needn't reach their ends.
Inputs may be any that keep to these rules, and one draw needn't show every extreme that they name: `band_index`: each entry is 64 * k + l with k and l below 32; the 128 entries of one block are distinct and the first is 0.
All inputs are finite; a program needn't handle non-finite values.
Results may differ from the reference program's by a relative error of at most 0.0003.
Values may be sent and summed in bfloat16 or wider, within the bound.
A program may use at most 192 MiB of HBM per device.

```python
import jax
import jax.numpy as jnp
from jax import lax

D = 8192
KVW = 512
CH = 64
BAND = 128
TOK_DEV = 768
TOKENS = 196608
N_REP = 4
N_FSDP = 64


def draw_band_index(key, part):
    key = jax.random.fold_in(key, 11)
    half = CH // 2
    block_count = D // CH * (KVW // CH)
    keys = jax.random.split(key, block_count)

    def one_block(block_key):
        first_key, second_key = jax.random.split(block_key)
        middle = jax.random.permutation(first_key, half * half - 2)[:BAND - 2].astype(jnp.int32) + 1
        top = jnp.full((1,), half * half - 1, jnp.int32)
        chosen = jnp.concatenate([middle, top])
        return jax.random.permutation(second_key, chosen).astype(jnp.int32)
    picks = jax.vmap(one_block)(keys)
    picks = jnp.concatenate([jnp.zeros((block_count, 1), jnp.int32), picks], axis=1)
    placed = picks // half * CH + picks % half
    return placed.reshape(D // CH, KVW // CH, BAND).astype(jnp.int32)


def raised(array, own_key, source, target, blocks, factor):
    def block_of(dim):
        return (jnp.arange(array.shape[dim]) // (array.shape[dim] // blocks)).reshape((-1,) + (1,) * (array.ndim - 1 - dim))

    near = jax.random.permutation(own_key, blocks)[block_of(target)]
    second = (block_of(target) + blocks // 2) % blocks
    return jnp.where((block_of(source) == near) | (block_of(source) == second), factor * array, array)


def levels(own_key, shape, shards, low, largest):
    def one(position, blocks):
        steps = jax.random.uniform(jax.random.fold_in(jax.random.fold_in(own_key, 6), position), (blocks,), jnp.float32, low / len(shards), largest / len(shards))
        return jnp.repeat(jnp.exp(steps), shape[position] // blocks).reshape((-1,) + (1,) * (len(shape) - position - 1))

    level = one(*shards[0])
    for cut in shards[1:]:
        level = level * one(*cut)
    return level


def scatter_about(stream_key, dims, scale, limit, cuts=(), kind=jnp.bfloat16):
    drawn = scale * jax.random.normal(stream_key, dims, jnp.float32)
    if cuts:
        drawn = drawn * levels(stream_key, dims, cuts, -0.22, 0.18)
    return jnp.clip(drawn, -limit, limit).astype(kind)


def noise_with(own_key, extent, deviation, most, pieces, heavy, kind=jnp.bfloat16):
    entries = deviation * jax.random.normal(own_key, extent, jnp.float32)
    if pieces:
        entries = entries * levels(own_key, extent, pieces, -0.22, 0.18)
    return jnp.clip(raised(entries, jax.random.fold_in(own_key, 3), *heavy), -most, most).astype(kind)


def setup_inputs(seed: int = 0) -> dict:
    key_list = jax.random.split(jax.random.key(seed), 6)
    return {
        "acts": noise_with(key_list[0], (TOKENS, D), 1.0, 24.0, ((0, 256),), (0, 1, 256, 6.0)),
        "cotangent": scatter_about(key_list[1], (TOKENS, KVW), (TOK_DEV * N_FSDP) ** -0.5, 0.02734375, ((0, 256),)),
        "momentum": scatter_about(key_list[2], (N_REP, D, KVW), 1.0, 6.0, ((0, 4), (1, 64)), jnp.float32),
        "params": scatter_about(key_list[3], (D, KVW), 0.1, 0.6, ((0, 64),), jnp.float32),
        "band_index": draw_band_index(jax.random.fold_in(key_list[5], 71), 0),
    }


beta_decay = 0.9
step_rate = 0.1
soft_width = 0.05

def dct_basis(size):
    freq = jnp.arange(size, dtype=jnp.float32)[:, None]
    cell = jnp.arange(size, dtype=jnp.float32)[None, :]
    weight = jnp.where(freq == 0, jnp.sqrt(1.0 / size), jnp.sqrt(2.0 / size))
    return weight * jnp.cos(jnp.pi * (2.0 * cell + 1.0) * freq / (2.0 * size))

def encode(field, basis):
    height, breadth = field.shape
    blocks = field.reshape(height // CH, CH, breadth // CH, CH)
    coeffs = jnp.einsum('ki,aibj,lj->abkl', basis, blocks, basis, precision=lax.Precision.HIGHEST)
    return coeffs.reshape(height // CH, breadth // CH, CH * CH)

def decode(flat, basis):
    first_n, second_n = (flat.shape[0], flat.shape[1])
    coeffs = flat.reshape(first_n, second_n, CH, CH)
    field = jnp.einsum('ki,abkl,lj->aibj', basis, coeffs, basis, precision=lax.Precision.HIGHEST)
    return field.reshape(first_n * CH, second_n * CH)

def place_band(values, band_index):
    first_n, second_n = (values.shape[0], values.shape[1])
    empty = jnp.zeros((first_n, second_n, CH * CH), values.dtype)
    first_axis = jnp.arange(first_n, dtype=jnp.int32)[:, None, None]
    second_axis = jnp.arange(second_n, dtype=jnp.int32)[None, :, None]
    return empty.at[first_axis, second_axis, band_index].set(values)

def reference(acts, cotangent, momentum, params, band_index):
    basis = dct_basis(CH)
    per_replica = TOK_DEV * N_FSDP
    moment_list = []
    band_list = []
    for replica in range(N_REP):
        inputs = acts[replica * per_replica:(replica + 1) * per_replica]
        outputs = cotangent[replica * per_replica:(replica + 1) * per_replica]
        gradient = lax.dot_general(inputs, outputs, (((0,), (0,)), ((), ())), preferred_element_type=jnp.float32)
        mixed = beta_decay * momentum[replica] + gradient
        coeffs = encode(mixed, basis)
        band_values = jnp.take_along_axis(coeffs, band_index, axis=2)
        moment_list.append(mixed - decode(place_band(band_values, band_index), basis))
        band_list.append(band_values)
    shared = lax.optimization_barrier(jnp.sum(jnp.stack(band_list), axis=0)) / N_REP
    decoded = decode(place_band(shared, band_index), basis)
    update = decoded / jnp.sqrt(decoded * decoded + soft_width * soft_width)
    new_params = params - step_rate * update
    return (jnp.stack(moment_list), new_params)
```

```python
import functools

import jax
import jax.numpy as jnp
import numpy as np
from jax import lax
from jax.experimental import pallas as pl
from jax.experimental.pallas import tpu as pltpu
from jax.sharding import PartitionSpec as P

MESH = pl.DeviceIdType.MESH
CH = 64
BAND = 128
ROWS = 128
KVW = 512
TOK = 768
HALF = KVW // 2
MSG = HALF + 16
TOP = 32000.0
beta_decay = 0.9
step_rate = 0.1
soft_width = 0.05
F32 = jnp.float32
BF16 = jnp.bfloat16


def basis_t():
    k = np.arange(CH)[:, None]
    i = np.arange(CH)[None, :]
    w = np.where(k == 0, np.sqrt(1.0 / CH), np.sqrt(2.0 / CH))
    return (w * np.cos(np.pi * (2 * i + 1) * k / (2 * CH))).T.astype(np.float32)


def pack(out, slot, val):
    top = jnp.maximum(jnp.max(jnp.abs(val), axis=0, keepdims=True), 1e-30)
    code = jnp.ceil(jnp.log(top) * 32.0)
    inv = TOP * jnp.exp(code * (-1.0 / 32.0))
    out[slot, 0:HALF, :] = jnp.round(val * inv).astype(jnp.int32).astype(jnp.int16)
    out[slot, HALF:MSG, :] = jnp.broadcast_to(code, (16, 128)).astype(jnp.int32).astype(jnp.int16)


def unpack(buf, slot):
    code = buf[slot, HALF:MSG, :].astype(jnp.int32).astype(F32)[0:1, :]
    scale = jnp.exp(code * (1.0 / 32.0)) * (1.0 / TOP)
    return buf[slot, 0:HALF, :].astype(jnp.int32).astype(F32) * scale


def split(x):
    hi = x.astype(BF16)
    lo = (x - hi.astype(F32)).astype(BF16)
    return hi, lo


def kernel(acts, cot, mom, par, band, bt, o_mom, o_par,
           abuf, craw, ct, part, sa, ra, sb, rb, sa2, ra2, sb2, rb2, sz, rz,
           acc, w_hi, w_lo, ksel, idx, btv, momv, parv, mixed, outv, vsum,
           vrecv,
           loc, dd_s, dd_r, co_s, co_r, misc,
           sem_sa, sem_ra, sem_sb, sem_rb, sem_sa2, sem_ra2, sem_sb2, sem_rb2,
           sem_sz, sem_rz, sem_sv, sem_rv):
    f = lax.axis_index("fsdp")
    rep = lax.axis_index("rep")
    x, zh = lax.div(f, 16), lax.rem(lax.div(f, 8), 2)
    y, c = lax.rem(lax.div(f, 2), 4), lax.rem(f, 2)

    def fid(xx, zz, yy, cc):
        return ((xx * 2 + zz) * 4 + yy) * 2 + cc

    def px(d):
        return fid(lax.rem(x + d, 4), zh, y, c)

    def py(d):
        return fid(x, zh, lax.rem(y + d, 4), c)

    pz = fid(x, 1 - zh, y, c)
    pc = fid(x, zh, y, 1 - c)

    def remote(src, dst, s, r, dev):
        return pltpu.make_async_remote_copy(src, dst, s, r, device_id={"fsdp": dev}, device_id_type=MESH)

    def column(p, h, core):
        w, s, i = lax.div(p, 8), lax.rem(lax.div(p, 4), 2), lax.rem(p, 4)
        dx = lax.rem(6 - i, 4)
        dy = 2 - 2 * h + s * (4 * h - 1)
        zd = lax.rem(zh + 1 - w + 2, 2)
        return pl.multiple_of(fid(lax.rem(x + dx, 4), zd, lax.rem(y + dy, 4), core) * ROWS, ROWS)

    def own_copy(p, h):
        return pltpu.make_async_copy(acts.at[:, pl.ds(column(p, h, c), ROWS)],
                                     abuf.at[p, pl.ds(0, TOK), pl.ds(h * ROWS, ROWS)], loc.at[2 * p + h])

    def core_copy(p, h):
        return remote(acts.at[:, pl.ds(column(p, h, 1 - c), ROWS)],
                      abuf.at[p, pl.ds(TOK, TOK), pl.ds(h * ROWS, ROWS)], dd_s.at[2 * p + h], dd_r.at[2 * p + h], pc)

    cot_in = pltpu.make_async_copy(cot, craw.at[pl.ds(0, TOK)], misc.at[0])
    cot_in.start()
    small = [pltpu.make_async_copy(band, idx, misc.at[1]), pltpu.make_async_copy(bt, btv, misc.at[2]),
             pltpu.make_async_copy(mom.at[0], momv, misc.at[3]), pltpu.make_async_copy(par, parv, misc.at[4])]

    barrier = pltpu.get_barrier_semaphore()
    for dev in (pc, px(1), px(2), px(3), py(1), py(2), py(3), pz):
        pl.semaphore_signal(barrier, inc=1, device_id={"fsdp": dev}, device_id_type=MESH)
    for d in (1, 2, 3):
        pl.semaphore_signal(barrier, inc=1, device_id={"rep": lax.rem(rep + d, 4)}, device_id_type=MESH)
    for cp in small:
        cp.start()

    @pl.loop(0, 16)
    def _(p):
        own_copy(p, 0).start()
        own_copy(p, 1).start()

    pl.semaphore_wait(barrier, 11)
    cot_over = remote(cot, craw.at[pl.ds(TOK, TOK)], co_s, co_r, pc)
    cot_over.start()

    @pl.loop(0, 16)
    def _(p):
        core_copy(p, 0).start()
        core_copy(p, 1).start()

    cot_in.wait()
    ct[:, 0:TOK] = craw[0:TOK, :].T
    small[0].wait()
    small[1].wait()

    b_hi, b_lo = split(btv[...])
    b2 = jnp.concatenate([b_hi, b_lo], axis=0)
    rowid = lax.broadcasted_iota(jnp.int32, (CH, BAND), 0)

    @pl.loop(0, 8)
    def _(g):
        b, jp = lax.div(g, 4), lax.rem(g, 4)
        w_hi[g] = jnp.zeros((128, 256), BF16)
        w_lo[g] = jnp.zeros((128, 256), BF16)
        for t in range(2):
            at = idx[b, pl.ds(2 * jp + t, 1), :]
            k1 = jnp.where(rowid == jnp.right_shift(at, 6), 1.0, 0.0).astype(BF16)
            l1 = jnp.where(rowid == jnp.bitwise_and(at, 63), 1.0, 0.0).astype(BF16)
            sel = jnp.dot(b2, jnp.concatenate([k1, l1], axis=1), preferred_element_type=F32)
            ksel[g, :, 128 * t:128 * t + 128] = sel[0:64, 0:128] + sel[64:128, 0:128]
            w_hi[g, 64 * t:64 * t + 64, 128 * t:128 * t + 128] = sel[0:64, 128:256].astype(BF16)
            w_lo[g, 64 * t:64 * t + 64, 128 * t:128 * t + 128] = sel[64:128, 128:256].astype(BF16)

    cot_over.wait_recv()
    ct[:, TOK:2 * TOK] = craw[TOK:2 * TOK, :].T

    def copy_a(slot, d):
        return remote(sa.at[slot], ra.at[slot], sem_sa.at[slot], sem_ra.at[slot], px(d))

    def copy_b(slot, d):
        return remote(sb.at[slot], rb.at[slot], sem_sb.at[slot], sem_rb.at[slot], py(d))

    def half(which, slot):
        p, h = lax.div(slot, 2), lax.rem(slot, 2)
        return part[p, pl.ds(which * HALF, HALF), pl.ds(pl.multiple_of(h * ROWS, ROWS), ROWS)]

    def produce(p):
        s, i = lax.rem(lax.div(p, 4), 2), lax.rem(p, 4)
        for h in range(2):
            own_copy(p, h).wait()
            core_copy(p, h).wait_recv()
        part[p] = jnp.dot(ct[...], abuf[p], preferred_element_type=F32)
        for h in range(2):
            slot = 2 * p + h
            if h == 0:
                go_a, da = lax.rem(i, 3) == 0, 1 + 2 * lax.div(i, 3)
                go_b, db = s * (1 - lax.rem(i, 2)) == 0, 1 + 2 * lax.rem(i, 2) * (1 - s)
            else:
                go_a, da = i < 2, 3 - 2 * i
                go_b, db = s * (1 - lax.rem(i, 2)) == 1, 3

            @pl.when(go_a)
            def _():
                pack(sa, slot, part[p, 0:HALF, h * ROWS:(h + 1) * ROWS])
                copy_a(slot, da).start()

            @pl.when(go_b)
            def _():
                pack(sb, slot, part[p, HALF:KVW, h * ROWS:(h + 1) * ROWS])
                copy_b(slot, db).start()

    def relay_a(w, s):
        @pl.loop(0, 2)
        def _(h):
            got = 16 * w + 8 * s + h
            slot = got + 2 + 4 * h
            copy_a(got, 1).wait_recv()
            pack(sa, slot, unpack(ra, got) + half(0, slot))
            copy_a(slot, 1 + 2 * h).start()

    def relay_b(w):
        @pl.loop(0, 4)
        def _(i):
            odd = lax.rem(i, 2)
            got = 16 * w + 2 * i
            slot = got + 8 + odd
            copy_b(got, 1).wait_recv()
            pack(sb, slot, unpack(rb, got) + half(1, slot))
            copy_b(slot, 1 + 2 * odd).start()

    def second_a(w, q):
        return remote(sa2.at[4 * w + q], ra2.at[4 * w + q], sem_sa2.at[4 * w + q], sem_ra2.at[4 * w + q],
                      py(lax.rem(2 + 2 * lax.rem(q, 2) + lax.div(q, 2) * (3 + 4 * lax.rem(q, 2)), 4)))

    def second_b(w, i):
        return remote(sb2.at[4 * w + i], rb2.at[4 * w + i], sem_sb2.at[4 * w + i], sem_rb2.at[4 * w + i],
                      px(lax.rem(6 - i, 4)))

    def first_sum(w):
        @pl.loop(0, 4)
        def _(q):
            s, h = lax.div(q, 2), lax.rem(q, 2)
            base = 16 * w + 8 * s + h
            copy_a(base + 2, 1).wait_recv()
            copy_a(base + 6, 1).wait_recv()
            total = half(0, base + 4) + unpack(ra, base + 2) + unpack(ra, base + 6)

            @pl.when(q == 1)
            def _():
                acc[2 * w] = total

            @pl.when(q != 1)
            def _():
                pack(sa2, 4 * w + q, total)
                second_a(w, q).start()

            got = 16 * w + 8 + 2 * q
            copy_b(got, 1).wait_recv()
            copy_b(got + 1, 1).wait_recv()
            total_b = half(1, 16 * w + 2 * q + 1) + unpack(rb, got) + unpack(rb, got + 1)

            @pl.when(q == 2)
            def _():
                acc[2 * w + 1] = total_b

            @pl.when(q != 2)
            def _():
                pack(sb2, 4 * w + q, total_b)
                second_b(w, q).start()

    def second_sum(w):
        for q in (0, 2, 3):
            second_a(w, q).wait_recv()
        ga = acc[2 * w] + unpack(ra2, 4 * w) + unpack(ra2, 4 * w + 2) + unpack(ra2, 4 * w + 3)
        for q in (0, 1, 3):
            second_b(w, q).wait_recv()
        gb = acc[2 * w + 1] + unpack(rb2, 4 * w) + unpack(rb2, 4 * w + 1) + unpack(rb2, 4 * w + 3)
        return ga, gb

    cross = [remote(sz.at[n], rz.at[n], sem_sz.at[n], sem_rz.at[n], pz) for n in range(2)]

    def produce_range(a, b):
        @pl.loop(a, b)
        def _(p):
            produce(p)

    produce_range(0, 6)
    relay_a(0, 0)
    produce_range(6, 8)
    relay_b(0)
    produce_range(8, 10)
    relay_a(0, 1)
    produce_range(10, 14)
    first_sum(0)
    produce_range(14, 16)
    relay_a(1, 0)
    relay_b(1)
    relay_a(1, 1)
    ga, gb = second_sum(0)
    pack(sz, 0, ga)
    cross[0].start()
    pack(sz, 1, gb)
    cross[1].start()
    first_sum(1)
    ga, gb = second_sum(1)
    small[2].wait()
    small[3].wait()
    cross[0].wait_recv()
    ga = ga + unpack(rz, 0)
    mixed[:, 0:HALF] = beta_decay * momv[:, 0:HALF] + ga.T
    cross[1].wait_recv()
    gb = gb + unpack(rz, 1)
    mixed[:, HALF:KVW] = beta_decay * momv[:, HALF:KVW] + gb.T

    def group(g):
        b, jp = g // 4, g % 4
        return slice(64 * b, 64 * b + 64), slice(128 * jp, 128 * jp + 128)

    for g in range(8):
        rows, cols = group(g)
        hi, lo = split(mixed[rows, cols])
        q = (jnp.dot(hi, w_hi[g], preferred_element_type=F32) + jnp.dot(lo, w_hi[g], preferred_element_type=F32)
             + jnp.dot(hi, w_lo[g], preferred_element_type=F32))
        vsum[g:g + 1, :] = jnp.sum(q * ksel[g], axis=0, keepdims=True)

    swap = [pltpu.make_async_remote_copy(vsum, vrecv.at[d - 1], sem_sv.at[d - 1], sem_rv.at[d - 1],
                                         device_id={"rep": lax.rem(rep + d, 4)}, device_id_type=MESH)
            for d in (1, 2, 3)]
    for cp in swap:
        cp.start()

    def nt(a, b):
        return lax.dot_general(a, b, (((1,), (1,)), ((), ())), preferred_element_type=F32)

    def decode(values, g):
        hi, lo = split(ksel[g] * values)
        return nt(hi, w_hi[g]) + nt(lo, w_hi[g]) + nt(hi, w_lo[g])

    for g in range(8):
        rows, cols = group(g)
        mixed[rows, cols] = mixed[rows, cols] - decode(vsum[g:g + 1, :], g)
    out_m = pltpu.make_async_copy(mixed, o_mom.at[0], misc.at[5])
    out_m.start()

    for cp in swap:
        cp.wait_recv()
    shared = (vsum[...] + vrecv[0] + vrecv[1] + vrecv[2]) * 0.25
    for g in range(8):
        rows, cols = group(g)
        d = decode(shared[g:g + 1, :], g)
        outv[rows, cols] = parv[rows, cols] - step_rate * (d * lax.rsqrt(d * d + soft_width * soft_width))
    out_p = pltpu.make_async_copy(outv, o_par, misc.at[6])
    out_p.start()

    @pl.loop(0, 32)
    def _(slot):
        p, h = lax.div(slot, 2), lax.rem(slot, 2)
        s, i = lax.rem(lax.div(p, 4), 2), lax.rem(p, 4)
        core_copy(p, h).wait_send()

        @pl.when(i != 2)
        def _():
            copy_a(slot, 1).wait_send()

        @pl.when(h * (1 - s) == 0)
        def _():
            copy_b(slot, 1).wait_send()

    for w in range(2):
        for q in (0, 2, 3):
            second_a(w, q).wait_send()
        for q in (0, 1, 3):
            second_b(w, q).wait_send()
    for cp in cross + swap + [cot_over]:
        cp.wait_send()
    out_m.wait()
    out_p.wait()


def per_device(acts, cotangent, momentum, params, band_index):
    any_ = pl.BlockSpec(memory_space=pl.ANY)
    dma = pltpu.SemaphoreType.DMA
    i16 = jnp.int16
    return pl.pallas_call(
        kernel,
        out_shape=(jax.ShapeDtypeStruct((1, ROWS, KVW), F32), jax.ShapeDtypeStruct((ROWS, KVW), F32)),
        in_specs=[any_] * 6,
        out_specs=(any_, any_),
        scratch_shapes=[
            pltpu.VMEM((16, 2 * TOK, 2 * ROWS), BF16),
            pltpu.VMEM((2 * TOK, KVW), BF16),
            pltpu.VMEM((KVW, 2 * TOK), BF16),
            pltpu.VMEM((16, KVW, 2 * ROWS), F32),
            pltpu.VMEM((32, MSG, 128), i16), pltpu.VMEM((32, MSG, 128), i16),
            pltpu.VMEM((32, MSG, 128), i16), pltpu.VMEM((32, MSG, 128), i16),
            pltpu.VMEM((8, MSG, 128), i16), pltpu.VMEM((8, MSG, 128), i16),
            pltpu.VMEM((8, MSG, 128), i16), pltpu.VMEM((8, MSG, 128), i16),
            pltpu.VMEM((2, MSG, 128), i16), pltpu.VMEM((2, MSG, 128), i16),
            pltpu.VMEM((4, HALF, 128), F32),
            pltpu.VMEM((8, 128, 256), BF16), pltpu.VMEM((8, 128, 256), BF16),
            pltpu.VMEM((8, 64, 256), F32),
            pltpu.VMEM((2, 8, 128), jnp.int32),
            pltpu.VMEM((CH, CH), F32),
            pltpu.VMEM((ROWS, KVW), F32), pltpu.VMEM((ROWS, KVW), F32),
            pltpu.VMEM((ROWS, KVW), F32), pltpu.VMEM((ROWS, KVW), F32),
            pltpu.VMEM((8, 256), F32), pltpu.VMEM((3, 8, 256), F32),
            dma((32,)), dma((32,)), dma((32,)), dma, dma, dma((7,)),
            dma((32,)), dma((32,)), dma((32,)), dma((32,)),
            dma((8,)), dma((8,)), dma((8,)), dma((8,)),
            dma((2,)), dma((2,)), dma((3,)), dma((3,)),
        ],
        compiler_params=pltpu.CompilerParams(collective_id=0, has_side_effects=True, vmem_limit_bytes=56 * 2**20),
        name="step",
    )(acts, cotangent, momentum, params, band_index, jnp.asarray(basis_t()))


def solution(mesh):
    return jax.shard_map(
        per_device,
        mesh=mesh,
        in_specs=(
            P(("rep", "fsdp"), None),
            P(("rep", "fsdp"), None),
            P("rep", "fsdp", None),
            P("fsdp", None),
            P("fsdp", None, None),
        ),
        out_specs=(P("rep", "fsdp", None), P("fsdp", None)),
        check_vma=False,
    )
```

```python
import functools

import jax
import jax.numpy as jnp
import numpy as np
from jax import lax
from jax.experimental import pallas as pl
from jax.experimental.pallas import tpu as pltpu
from jax.sharding import PartitionSpec as P

MESH = pl.DeviceIdType.MESH
CH = 64
BAND = 128
ROWS = 128
KVW = 512
TOK = 768
HALF = KVW // 2
TOP = 32000.0
A1, B1, A2, B2, Z = 0, 32, 64, 72, 80
N_MSG = 82
N_GROUP = 38
beta_decay = 0.9
step_rate = 0.1
soft_width = 0.05
F32 = jnp.float32
BF16 = jnp.bfloat16


def basis_t():
    i = lax.broadcasted_iota(jnp.int32, (CH, CH), 0)
    k = lax.broadcasted_iota(jnp.int32, (CH, CH), 1)
    turn = jnp.bitwise_and((2 * i + 1) * k, 4 * CH - 1).astype(F32)
    return jnp.where(k == 0, (1.0 / CH) ** 0.5, (2.0 / CH) ** 0.5) * jnp.cos(turn * (np.pi / (2 * CH)))


def pack(out, scales, slot, val):
    scale = jnp.maximum(jnp.max(jnp.abs(val), axis=0, keepdims=True), 1e-30) * (1.0 / TOP)
    out[slot] = jnp.round(val * (1.0 / scale)).astype(jnp.int32).astype(jnp.int16)
    scales[slot] = scale


def unpack(buf, scales, slot):
    return buf[slot].astype(jnp.int32).astype(F32) * scales[slot]


def split(x):
    hi = x.astype(BF16)
    lo = (x - hi.astype(F32)).astype(BF16)
    return hi, lo


def kernel(acts, cot, mom, band, mixed, own, out,
           abuf, craw, ct, part, sbuf, rbuf, sscale, rscale,
           acc, w_hi, w_lo, ksel, idx, momv, vsum, vrecv,
           loc, dd_s, dd_r, co_s, co_r, misc, sem_s, sem_r, sem_ss, sem_rs, sem_sv, sem_rv):
    f = lax.axis_index("fsdp")
    rep = lax.axis_index("rep")
    x, zh = lax.div(f, 16), lax.rem(lax.div(f, 8), 2)
    y, c = lax.rem(lax.div(f, 2), 4), lax.rem(f, 2)

    def fid(xx, zz, yy, cc):
        return ((xx * 2 + zz) * 4 + yy) * 2 + cc

    def px(d):
        return fid(lax.rem(x + d, 4), zh, y, c)

    def py(d):
        return fid(x, zh, lax.rem(y + d, 4), c)

    pz = fid(x, 1 - zh, y, c)
    pc = fid(x, zh, y, 1 - c)

    def remote(src, dst, s, r, dev):
        return pltpu.make_async_remote_copy(src, dst, s, r, device_id={"fsdp": dev}, device_id_type=MESH)

    def column(p, h, core):
        w, s, i = lax.div(p, 8), lax.rem(lax.div(p, 4), 2), lax.rem(p, 4)
        dx = lax.rem(6 - i - lax.div(i, 2) * (1 - 2 * lax.rem(i, 2)), 4)
        dy = 2 - h + s * (1 - 2 * h)
        zd = lax.rem(zh + 3 - w, 2)
        return pl.multiple_of(fid(lax.rem(x + dx, 4), zd, lax.rem(y + dy, 4), core) * ROWS, ROWS)

    def own_copy(p, h, sem):
        return pltpu.make_async_copy(acts.at[:, pl.ds(column(p, h, c), ROWS)],
                                     abuf.at[p, pl.ds(0, TOK), pl.ds(h * ROWS, ROWS)], loc.at[sem])

    def core_copy(p, h):
        return remote(acts.at[:, pl.ds(column(p, h, 1 - c), ROWS)],
                      abuf.at[p, pl.ds(TOK, TOK), pl.ds(h * ROWS, ROWS)], dd_s, dd_r.at[p], pc)

    cot_in = pltpu.make_async_copy(cot, craw.at[pl.ds(0, TOK)], misc.at[0])
    band_in = pltpu.make_async_copy(band, idx, misc.at[1])
    mom_in = pltpu.make_async_copy(mom.at[0], momv, misc.at[2])
    cot_over = [remote(cot.at[:, pl.ds(HALF * n, HALF)], craw.at[pl.ds(TOK, TOK), pl.ds(HALF * n, HALF)],
                       co_s, co_r.at[n], pc) for n in range(2)]

    barrier = pltpu.get_barrier_semaphore()
    for dev in (pc, px(1), px(2), px(3), py(1), py(2), py(3), pz):
        pl.semaphore_signal(barrier, inc=1, device_id={"fsdp": dev}, device_id_type=MESH)
    for d in (1, 2, 3):
        pl.semaphore_signal(barrier, inc=1, device_id={"rep": lax.rem(rep + d, 4)}, device_id_type=MESH)
    cot_in.start()
    own_copy(0, 0, 0).start()
    own_copy(0, 1, 0).start()
    pl.semaphore_wait(barrier, 11)
    cot_over[0].start()
    core_copy(0, 0).start()
    core_copy(0, 1).start()
    cot_over[1].start()
    band_in.start()
    mom_in.start()

    for sem, (a, b) in enumerate(((1, 6), (6, 16))):
        @pl.loop(a, b)
        def _(p):
            for h in range(2):
                core_copy(p, h).start()
                own_copy(p, h, sem + 1).start()

    cot_in.wait()
    ct[:, 0:TOK] = craw[0:TOK, :].T
    band_in.wait()

    b_hi, b_lo = split(basis_t())
    b2 = jnp.concatenate([b_hi, b_lo], axis=0)
    rowid = lax.broadcasted_iota(jnp.int32, (CH, BAND), 0)

    @pl.loop(0, 8)
    def _(g):
        b, jp = lax.div(g, 4), lax.rem(g, 4)
        w_hi[g] = jnp.zeros((128, 256), BF16)
        w_lo[g] = jnp.zeros((128, 256), BF16)
        for t in range(2):
            at = idx[b, pl.ds(2 * jp + t, 1), :]
            k1 = jnp.where(rowid == jnp.right_shift(at, 6), 1.0, 0.0).astype(BF16)
            l1 = jnp.where(rowid == jnp.bitwise_and(at, 63), 1.0, 0.0).astype(BF16)
            sel = jnp.dot(b2, jnp.concatenate([k1, l1], axis=1), preferred_element_type=F32)
            ksel[g, :, 128 * t:128 * t + 128] = sel[0:64, 0:128] + sel[64:128, 0:128]
            w_hi[g, 64 * t:64 * t + 64, 128 * t:128 * t + 128] = sel[0:64, 128:256].astype(BF16)
            w_lo[g, 64 * t:64 * t + 64, 128 * t:128 * t + 128] = sel[64:128, 128:256].astype(BF16)

    def take(group, *slots):
        n = pl.ds(0, len(slots))
        remote(rbuf.at[n], rbuf.at[n], sem_s, sem_r.at[group], pz).wait_recv()
        remote(rscale.at[n], rscale.at[n], sem_ss, sem_rs.at[group], pz).wait_recv()
        return sum(unpack(rbuf, rscale, slot) for slot in slots)

    def send(slot, group, dev, val):
        pack(sbuf, sscale, slot, val)
        remote(sbuf.at[slot], rbuf.at[slot], sem_s, sem_r.at[group], dev).start()
        remote(sscale.at[slot], rscale.at[slot], sem_ss, sem_rs.at[group], dev).start()

    def send_a1(slot, d, val):
        p, h = lax.div(slot, 2), lax.rem(slot, 2)
        send(A1 + slot, 2 * lax.div(p, 4) + h + 8 * lax.div(lax.rem(p, 4) + 3, 4), px(d), val)

    def send_b1(slot, d, val):
        p, h = lax.div(slot, 2), lax.rem(slot, 2)
        w, s, i = lax.div(p, 8), lax.rem(lax.div(p, 4), 2), lax.rem(p, 4)
        send(B1 + slot, 24 + 4 * w + i - 8 * (1 - s) * (1 - h), py(d), val)

    def send_2(n, w, q, val):
        to = (py, px)[n](2 - q + 3 * lax.div(q, 2))
        send((A2, B2)[n] + 4 * w + q, 32 + 2 * n + w, to, val)

    def half(which, slot):
        p, h = lax.div(slot, 2), lax.rem(slot, 2)
        return part[p, pl.ds(which * HALF, HALF), pl.ds(pl.multiple_of(h * ROWS, ROWS), ROWS)]

    def send_a(p):
        i = lax.rem(p, 4)
        for h in range(2):
            go, d = (lax.rem(i, 2) == 0, 1 + i) if h == 0 else (i < 2, 3 - 2 * i)

            @pl.when(go)
            def _():
                send_a1(2 * p + h, d, part[p, 0:HALF, h * ROWS:(h + 1) * ROWS])

    def send_b(p):
        s, odd = lax.rem(lax.div(p, 4), 2), lax.rem(p, 2)
        for h in range(2):
            go, d = (s * odd == 0, 1 + 2 * odd + 2 * s) if h == 0 else ((1 - s) * odd == 1, 1)

            @pl.when(go)
            def _():
                send_b1(2 * p + h, d, part[p, HALF:KVW, h * ROWS:(h + 1) * ROWS])

    def loaded(a, b, sem):
        there = abuf.at[pl.ds(a, b - a), pl.ds(0, TOK)]
        pltpu.make_async_copy(there, there, loc.at[sem]).wait()

    def arrive(p):
        there = abuf.at[p, pl.ds(TOK, TOK)]
        remote(there, there, dd_s, dd_r.at[p], pc).wait_recv()

    def produce(a, b):
        @pl.loop(a, b)
        def _(p):
            arrive(p)
            part[p] = jnp.dot(ct[...], abuf[p], preferred_element_type=F32)
            send_a(p)
            send_b(p)

    def relay_a(w, s):
        @pl.loop(0, 2)
        def _(h):
            got = 16 * w + 8 * s + h
            slot = got + 2 + 2 * h
            send_a1(slot, 1 + 2 * h, take(4 * w + 2 * s + h, A1 + got) + half(0, slot))

    def relay_b(w, a, b):
        @pl.loop(a, b)
        def _(i):
            odd = lax.rem(i, 2)
            got = 16 * w + 2 * i
            slot = got + 1 + 7 * odd
            send_b1(slot, 1 + 2 * odd, take(16 + 4 * w + i, B1 + got) + half(1, slot))

    def first_sum(w, a, b):
        @pl.loop(a, b)
        def _(q):
            base = 16 * w + 8 * lax.div(q, 2) + lax.rem(q, 2)
            total = half(0, base + 6) + take(8 + 4 * w + q, A1 + base + 2, A1 + base + 4)

            @pl.when(q == 3)
            def _():
                acc[2 * w] = total

            @pl.when(q != 3)
            def _():
                send_2(0, w, q, total)

            got = 16 * w + 2 * q
            total_b = half(1, got + 9) + take(24 + 4 * w + q, B1 + got + 1, B1 + got + 8)

            @pl.when(q == 3)
            def _():
                acc[2 * w + 1] = total_b

            @pl.when(q != 3)
            def _():
                send_2(1, w, q, total_b)

    def second_sum(w, n):
        at = (A2, B2)[n] + 4 * w
        return acc[2 * w + n] + take(32 + 2 * n + w, at, at + 1, at + 2)

    loaded(0, 1, 0)
    arrive(0)
    for n in range(2):
        cot_over[n].wait_recv()
        ct[HALF * n:HALF * n + HALF, TOK:2 * TOK] = craw[TOK:2 * TOK, HALF * n:HALF * n + HALF].T
        part[0, HALF * n:HALF * n + HALF, :] = jnp.dot(ct[HALF * n:HALF * n + HALF, :], abuf[0],
                                                       preferred_element_type=F32)
        (send_a, send_b)[n](jnp.int32(0))
    loaded(1, 6, 1)
    produce(1, 6)
    relay_a(0, 0)
    relay_b(0, 0, 3)
    loaded(6, 16, 2)
    produce(6, 8)
    relay_b(0, 3, 4)
    relay_a(0, 1)
    produce(8, 14)
    first_sum(0, 0, 4)
    produce(14, 16)
    relay_a(1, 0)
    relay_b(1, 0, 2)
    relay_a(1, 1)
    relay_b(1, 2, 4)
    for n in range(2):
        send(Z + n, 36 + n, pz, second_sum(0, n))
    first_sum(1, 0, 4)
    mom_in.wait()
    for n in range(2):
        total = second_sum(1, n) + take(36 + n, Z + n)
        cols = slice(HALF * n, HALF * n + HALF)
        mixed[:, cols] = beta_decay * momv[:, cols] + total.T

    def group(g):
        b, jp = g // 4, g % 4
        return slice(64 * b, 64 * b + 64), slice(128 * jp, 128 * jp + 128)

    for g in range(8):
        rows, cols = group(g)
        hi, lo = split(mixed[rows, cols])
        q = (jnp.dot(hi, w_hi[g], preferred_element_type=F32) + jnp.dot(lo, w_hi[g], preferred_element_type=F32)
             + jnp.dot(hi, w_lo[g], preferred_element_type=F32))
        vsum[g:g + 1, :] = jnp.sum(q * ksel[g], axis=0, keepdims=True)

    swap = [pltpu.make_async_remote_copy(vsum, vrecv.at[d - 1], sem_sv, sem_rv,
                                         device_id={"rep": lax.rem(rep + d, 4)}, device_id_type=MESH)
            for d in (1, 2, 3)]
    for cp in swap:
        cp.start()
    swapped = pltpu.make_async_remote_copy(vrecv, vrecv, sem_sv, sem_rv,
                                           device_id={"rep": lax.rem(rep + 1, 4)}, device_id_type=MESH)

    def nt(a, b):
        return lax.dot_general(a, b, (((1,), (1,)), ((), ())), preferred_element_type=F32)

    def decode(values, g):
        hi, lo = split(ksel[g] * values)
        return nt(hi, w_hi[g]) + nt(lo, w_hi[g]) + nt(hi, w_lo[g])

    for g in range(8):
        rows, cols = group(g)
        own[rows, cols] = decode(vsum[g:g + 1, :], g)

    swapped.wait_recv()
    shared = (vsum[...] + vrecv[0] + vrecv[1] + vrecv[2]) * 0.25
    for g in range(8):
        rows, cols = group(g)
        out[rows, cols] = decode(shared[g:g + 1, :], g)

    n = pl.ds(0, 62)
    remote(sbuf.at[n], rbuf.at[n], sem_s, sem_r.at[0], pz).wait_send()
    remote(sscale.at[n], rscale.at[n], sem_ss, sem_rs.at[0], pz).wait_send()
    there = abuf.at[:, pl.ds(0, TOK)]
    remote(there, there, dd_s, dd_r.at[0], pc).wait_send()
    there = craw.at[pl.ds(0, TOK)]
    remote(there, there, co_s, co_r.at[0], pc).wait_send()
    swapped.wait_send()


def per_device(acts, cotangent, momentum, params, band_index):
    any_ = pl.BlockSpec(memory_space=pl.ANY)
    dma = pltpu.SemaphoreType.DMA
    mixed, own, decoded = pl.pallas_call(
        kernel,
        out_shape=[jax.ShapeDtypeStruct((ROWS, KVW), F32)] * 3,
        in_specs=[any_] * 4,
        out_specs=[pl.BlockSpec(memory_space=pltpu.VMEM)] * 3,
        scratch_shapes=[
            pltpu.VMEM((16, 2 * TOK, 2 * ROWS), BF16),
            pltpu.VMEM((2 * TOK, KVW), BF16),
            pltpu.VMEM((KVW, 2 * TOK), BF16),
            pltpu.VMEM((16, KVW, 2 * ROWS), F32),
            pltpu.VMEM((N_MSG, HALF, 128), jnp.int16), pltpu.VMEM((N_MSG, HALF, 128), jnp.int16),
            pltpu.VMEM((N_MSG, 1, 128), F32), pltpu.VMEM((N_MSG, 1, 128), F32),
            pltpu.VMEM((4, HALF, 128), F32),
            pltpu.VMEM((8, 128, 256), BF16), pltpu.VMEM((8, 128, 256), BF16),
            pltpu.VMEM((8, 64, 256), F32),
            pltpu.VMEM((2, 8, 128), jnp.int32),
            pltpu.VMEM((ROWS, KVW), F32),
            pltpu.VMEM((8, 256), F32), pltpu.VMEM((3, 8, 256), F32),
            dma((3,)), dma, dma((16,)), dma, dma((2,)), dma((3,)),
            dma, dma((N_GROUP,)), dma, dma((N_GROUP,)), dma, dma,
        ],
        compiler_params=pltpu.CompilerParams(collective_id=0, has_side_effects=True, vmem_limit_bytes=53 * 2**20),
        name="step",
    )(acts, cotangent, momentum, band_index)
    update = decoded * lax.rsqrt(decoded * decoded + soft_width * soft_width)
    return (mixed - own)[None], params - step_rate * update


def solution(mesh):
    return jax.shard_map(
        per_device,
        mesh=mesh,
        in_specs=(
            P(("rep", "fsdp"), None),
            P(("rep", "fsdp"), None),
            P("rep", "fsdp", None),
            P("fsdp", None),
            P("fsdp", None, None),
        ),
        out_specs=(P("rep", "fsdp", None), P("fsdp", None)),
        check_vma=False,
    )
```

```python
import functools

import jax
import jax.numpy as jnp
import numpy as np
from jax import lax
from jax.experimental import pallas as pl
from jax.experimental.pallas import tpu as pltpu
from jax.sharding import PartitionSpec as P

MESH = pl.DeviceIdType.MESH
CH = 64
BAND = 128
ROWS = 128
KVW = 512
TOK = 768
HALF = KVW // 2
TOP = 32000.0
A1, B1, A2, B2, Z = 0, 32, 64, 72, 80
N_MSG = 82
N_GROUP = 38
beta_decay = 0.9
step_rate = 0.1
soft_width = 0.05
F32 = jnp.float32
BF16 = jnp.bfloat16


def basis_t():
    i = lax.broadcasted_iota(jnp.int32, (CH, CH), 0)
    k = lax.broadcasted_iota(jnp.int32, (CH, CH), 1)
    turn = jnp.bitwise_and((2 * i + 1) * k, 4 * CH - 1).astype(F32)
    return jnp.where(k == 0, (1.0 / CH) ** 0.5, (2.0 / CH) ** 0.5) * jnp.cos(turn * (np.pi / (2 * CH)))


def pack(out, scales, slot, val):
    scale = jnp.maximum(jnp.max(jnp.abs(val), axis=0, keepdims=True), 1e-30) * (1.0 / TOP)
    out[slot] = jnp.round(val * (1.0 / scale)).astype(jnp.int32).astype(jnp.int16)
    scales[slot] = scale


def unpack(buf, scales, slot):
    return buf[slot].astype(jnp.int32).astype(F32) * scales[slot]


def split(x):
    hi = x.astype(BF16)
    lo = (x - hi.astype(F32)).astype(BF16)
    return hi, lo


def kernel(acts, cot, mom, band, mixed, own, out,
           abuf, craw, ct, part, sbuf, rbuf, sscale, rscale,
           acc, w_hi, w_lo, ksel, idx, momv, vsum, vrecv,
           loc, dd_s, dd_r, co_s, co_r, misc, sem_s, sem_r, sem_ss, sem_rs, sem_sv, sem_rv, ready_z, ready_rep):
    f = lax.axis_index("fsdp")
    rep = lax.axis_index("rep")
    x, zh = lax.div(f, 16), lax.rem(lax.div(f, 8), 2)
    y, c = lax.rem(lax.div(f, 2), 4), lax.rem(f, 2)

    def fid(xx, zz, yy, cc):
        return ((xx * 2 + zz) * 4 + yy) * 2 + cc

    def px(d):
        return fid(lax.rem(x + d, 4), zh, y, c)

    def py(d):
        return fid(x, zh, lax.rem(y + d, 4), c)

    pz = fid(x, 1 - zh, y, c)
    pc = fid(x, zh, y, 1 - c)

    def remote(src, dst, s, r, dev):
        return pltpu.make_async_remote_copy(src, dst, s, r, device_id={"fsdp": dev}, device_id_type=MESH)

    def column(p, h, core):
        w, s, i = lax.div(p, 8), lax.rem(lax.div(p, 4), 2), lax.rem(p, 4)
        dx = lax.rem(6 - i - lax.div(i, 2) * (1 - 2 * lax.rem(i, 2)), 4)
        dy = 2 - h + s * (1 - 2 * h)
        zd = lax.rem(zh + 3 - w, 2)
        return pl.multiple_of(fid(lax.rem(x + dx, 4), zd, lax.rem(y + dy, 4), core) * ROWS, ROWS)

    def own_copy(p, h, sem):
        return pltpu.make_async_copy(acts.at[:, pl.ds(column(p, h, c), ROWS)],
                                     abuf.at[p, pl.ds(0, TOK), pl.ds(h * ROWS, ROWS)], loc.at[sem])

    def core_copy(p, h):
        return remote(acts.at[:, pl.ds(column(p, h, 1 - c), ROWS)],
                      abuf.at[p, pl.ds(TOK, TOK), pl.ds(h * ROWS, ROWS)], dd_s, dd_r.at[p], pc)

    cot_in = pltpu.make_async_copy(cot, craw.at[pl.ds(0, TOK)], misc.at[0])
    band_in = pltpu.make_async_copy(band, idx, misc.at[1])
    mom_in = pltpu.make_async_copy(mom.at[0], momv, misc.at[2])
    cot_over = [remote(cot.at[:, pl.ds(HALF * n, HALF)], craw.at[pl.ds(TOK, TOK), pl.ds(HALF * n, HALF)],
                       co_s, co_r.at[n], pc) for n in range(2)]

    barrier = pltpu.get_barrier_semaphore()
    for dev in (pc, px(1), px(2), px(3), py(1), py(2), py(3)):
        pl.semaphore_signal(barrier, inc=1, device_id={"fsdp": dev}, device_id_type=MESH)

    @pl.when(zh == 0)
    def _():
        pl.semaphore_signal(barrier, inc=1, device_id={"fsdp": pz}, device_id_type=MESH)

    for d in (1, 2, 3):
        @pl.when(rep + d < 4)
        def _():
            pl.semaphore_signal(barrier, inc=1, device_id={"rep": lax.rem(rep + d, 4)}, device_id_type=MESH)

    cot_in.start()
    own_copy(0, 0, 0).start()
    own_copy(0, 1, 0).start()
    pl.semaphore_wait(barrier, 7 + zh + rep)
    cot_over[0].start()
    core_copy(0, 0).start()
    core_copy(0, 1).start()
    cot_over[1].start()
    band_in.start()
    mom_in.start()

    @pl.when(zh == 1)
    def _():
        pl.semaphore_signal(ready_z, inc=1, device_id={"fsdp": pz}, device_id_type=MESH)

    for d in (1, 2, 3):
        @pl.when(rep >= d)
        def _():
            pl.semaphore_signal(ready_rep, inc=1, device_id={"rep": lax.rem(rep + 4 - d, 4)}, device_id_type=MESH)

    for sem, (a, b) in enumerate(((1, 6), (6, 16))):
        @pl.loop(a, b)
        def _(p):
            for h in range(2):
                core_copy(p, h).start()
                own_copy(p, h, sem + 1).start()

    cot_in.wait()
    ct[:, 0:TOK] = craw[0:TOK, :].T
    band_in.wait()

    b_hi, b_lo = split(basis_t())
    b2 = jnp.concatenate([b_hi, b_lo], axis=0)
    rowid = lax.broadcasted_iota(jnp.int32, (CH, BAND), 0)

    @pl.loop(0, 8)
    def _(g):
        b, jp = lax.div(g, 4), lax.rem(g, 4)
        w_hi[g] = jnp.zeros((128, 256), BF16)
        w_lo[g] = jnp.zeros((128, 256), BF16)
        for t in range(2):
            at = idx[b, pl.ds(2 * jp + t, 1), :]
            k1 = jnp.where(rowid == jnp.right_shift(at, 6), 1.0, 0.0).astype(BF16)
            l1 = jnp.where(rowid == jnp.bitwise_and(at, 63), 1.0, 0.0).astype(BF16)
            sel = jnp.dot(b2, jnp.concatenate([k1, l1], axis=1), preferred_element_type=F32)
            ksel[g, :, 128 * t:128 * t + 128] = sel[0:64, 0:128] + sel[64:128, 0:128]
            w_hi[g, 64 * t:64 * t + 64, 128 * t:128 * t + 128] = sel[0:64, 128:256].astype(BF16)
            w_lo[g, 64 * t:64 * t + 64, 128 * t:128 * t + 128] = sel[64:128, 128:256].astype(BF16)

    def take(group, *slots):
        n = pl.ds(0, len(slots))
        remote(rbuf.at[n], rbuf.at[n], sem_s, sem_r.at[group], pz).wait_recv()
        remote(rscale.at[n], rscale.at[n], sem_ss, sem_rs.at[group], pz).wait_recv()
        return sum(unpack(rbuf, rscale, slot) for slot in slots)

    def send(slot, group, dev, val):
        pack(sbuf, sscale, slot, val)
        remote(sbuf.at[slot], rbuf.at[slot], sem_s, sem_r.at[group], dev).start()
        remote(sscale.at[slot], rscale.at[slot], sem_ss, sem_rs.at[group], dev).start()

    def send_a1(slot, d, val):
        p, h = lax.div(slot, 2), lax.rem(slot, 2)
        send(A1 + slot, 2 * lax.div(p, 4) + h + 8 * lax.div(lax.rem(p, 4) + 3, 4), px(d), val)

    def send_b1(slot, d, val):
        p, h = lax.div(slot, 2), lax.rem(slot, 2)
        w, s, i = lax.div(p, 8), lax.rem(lax.div(p, 4), 2), lax.rem(p, 4)
        send(B1 + slot, 24 + 4 * w + i - 8 * (1 - s) * (1 - h), py(d), val)

    def send_2(n, w, q, val):
        to = (py, px)[n](2 - q + 3 * lax.div(q, 2))
        send((A2, B2)[n] + 4 * w + q, 32 + 2 * n + w, to, val)

    def half(which, slot):
        p, h = lax.div(slot, 2), lax.rem(slot, 2)
        return part[p, pl.ds(which * HALF, HALF), pl.ds(pl.multiple_of(h * ROWS, ROWS), ROWS)]

    def send_a(p):
        i = lax.rem(p, 4)
        for h in range(2):
            go, d = (lax.rem(i, 2) == 0, 1 + i) if h == 0 else (i + 2 * lax.div(p, 12) < 2, 3 - 2 * i)

            @pl.when(go)
            def _():
                send_a1(2 * p + h, d, part[p, 0:HALF, h * ROWS:(h + 1) * ROWS])

    def send_b(p):
        s, odd = lax.rem(lax.div(p, 4), 2), lax.rem(p, 2)
        last = lax.div(p, 11) - lax.div(p, 12)
        for h in range(2):
            go, d = (s * odd + last == 0, 1 + 2 * odd + 2 * s) if h == 0 else ((1 - s) * odd - last == 1, 1)

            @pl.when(go)
            def _():
                send_b1(2 * p + h, d, part[p, HALF:KVW, h * ROWS:(h + 1) * ROWS])

    def loaded(a, b, sem):
        there = abuf.at[pl.ds(a, b - a), pl.ds(0, TOK)]
        pltpu.make_async_copy(there, there, loc.at[sem]).wait()

    def arrive(p):
        there = abuf.at[p, pl.ds(TOK, TOK)]
        remote(there, there, dd_s, dd_r.at[p], pc).wait_recv()

    def produce(a, b):
        @pl.loop(a, b)
        def _(p):
            arrive(p)
            part[p] = jnp.dot(ct[...], abuf[p], preferred_element_type=F32)
            send_a(p)
            send_b(p)

    def late():
        send_a1(25, 3, part[12, 0:HALF, ROWS:2 * ROWS])
        send_b1(22, 3, part[11, HALF:KVW, 0:ROWS])
        send_a1(27, 1, part[13, 0:HALF, ROWS:2 * ROWS])
        send_b1(23, 1, part[11, HALF:KVW, ROWS:2 * ROWS])

    def relay_a(w, s, a=0, b=2):
        @pl.loop(a, b)
        def _(h):
            got = 16 * w + 8 * s + h
            slot = got + 2 + 2 * h
            send_a1(slot, 1 + 2 * h, take(4 * w + 2 * s + h, A1 + got) + half(0, slot))

    def relay_b(w, a, b):
        @pl.loop(a, b)
        def _(i):
            odd = lax.rem(i, 2)
            got = 16 * w + 2 * i
            slot = got + 1 + 7 * odd
            send_b1(slot, 1 + 2 * odd, take(16 + 4 * w + i, B1 + got) + half(1, slot))

    def first_sum(w, a, b):
        @pl.loop(a, b)
        def _(q):
            base = 16 * w + 8 * lax.div(q, 2) + lax.rem(q, 2)
            total = half(0, base + 6) + take(8 + 4 * w + q, A1 + base + 2, A1 + base + 4)

            @pl.when(q == 3)
            def _():
                acc[2 * w] = total

            @pl.when(q != 3)
            def _():
                send_2(0, w, q, total)

            got = 16 * w + 2 * q
            total_b = half(1, got + 9) + take(24 + 4 * w + q, B1 + got + 1, B1 + got + 8)

            @pl.when(q == 3)
            def _():
                acc[2 * w + 1] = total_b

            @pl.when(q != 3)
            def _():
                send_2(1, w, q, total_b)

    def second_sum(w, n):
        at = (A2, B2)[n] + 4 * w
        return acc[2 * w + n] + take(32 + 2 * n + w, at, at + 1, at + 2)

    loaded(0, 1, 0)
    arrive(0)
    for n in range(2):
        cot_over[n].wait_recv()
        ct[HALF * n:HALF * n + HALF, TOK:2 * TOK] = craw[TOK:2 * TOK, HALF * n:HALF * n + HALF].T
        part[0, HALF * n:HALF * n + HALF, :] = jnp.dot(ct[HALF * n:HALF * n + HALF, :], abuf[0],
                                                       preferred_element_type=F32)
        (send_a, send_b)[n](jnp.int32(0))
    loaded(1, 6, 1)
    produce(1, 6)
    relay_a(0, 0)
    relay_b(0, 0, 3)
    loaded(6, 16, 2)
    produce(6, 8)
    relay_b(0, 3, 4)
    relay_a(0, 1)
    produce(8, 14)
    first_sum(0, 0, 4)
    produce(14, 16)
    late()
    relay_a(1, 0)
    relay_b(1, 0, 3)
    relay_a(1, 1, 0, 1)
    @pl.when(zh == 0)
    def _():
        pl.semaphore_wait(ready_z, 1)

    for n in range(2):
        send(Z + n, 36 + n, pz, second_sum(0, n))
    relay_a(1, 1, 1, 2)
    relay_b(1, 3, 4)
    first_sum(1, 0, 4)
    mom_in.wait()
    for n in range(2):
        total = second_sum(1, n) + take(36 + n, Z + n)
        cols = slice(HALF * n, HALF * n + HALF)
        mixed[:, cols] = beta_decay * momv[:, cols] + total.T

    def group(g):
        b, jp = g // 4, g % 4
        return slice(64 * b, 64 * b + 64), slice(128 * jp, 128 * jp + 128)

    for g in range(8):
        rows, cols = group(g)
        hi, lo = split(mixed[rows, cols])
        q = (jnp.dot(hi, w_hi[g], preferred_element_type=F32) + jnp.dot(lo, w_hi[g], preferred_element_type=F32)
             + jnp.dot(hi, w_lo[g], preferred_element_type=F32))
        vsum[g:g + 1, :] = jnp.sum(q * ksel[g], axis=0, keepdims=True)

    @pl.when(rep < 3)
    def _():
        pl.semaphore_wait(ready_rep, 3 - rep)

    swap = [pltpu.make_async_remote_copy(vsum, vrecv.at[d - 1], sem_sv, sem_rv,
                                         device_id={"rep": lax.rem(rep + d, 4)}, device_id_type=MESH)
            for d in (1, 2, 3)]
    for cp in swap:
        cp.start()
    swapped = pltpu.make_async_remote_copy(vrecv, vrecv, sem_sv, sem_rv,
                                           device_id={"rep": lax.rem(rep + 1, 4)}, device_id_type=MESH)

    def nt(a, b):
        return lax.dot_general(a, b, (((1,), (1,)), ((), ())), preferred_element_type=F32)

    def decode(values, g):
        hi, lo = split(ksel[g] * values)
        return nt(hi, w_hi[g]) + nt(lo, w_hi[g]) + nt(hi, w_lo[g])

    for g in range(8):
        rows, cols = group(g)
        own[rows, cols] = decode(vsum[g:g + 1, :], g)

    swapped.wait_recv()
    shared = (vsum[...] + vrecv[0] + vrecv[1] + vrecv[2]) * 0.25
    for g in range(8):
        rows, cols = group(g)
        out[rows, cols] = decode(shared[g:g + 1, :], g)

    n = pl.ds(0, 62)
    remote(sbuf.at[n], rbuf.at[n], sem_s, sem_r.at[0], pz).wait_send()
    remote(sscale.at[n], rscale.at[n], sem_ss, sem_rs.at[0], pz).wait_send()
    there = abuf.at[:, pl.ds(0, TOK)]
    remote(there, there, dd_s, dd_r.at[0], pc).wait_send()
    there = craw.at[pl.ds(0, TOK)]
    remote(there, there, co_s, co_r.at[0], pc).wait_send()
    swapped.wait_send()


def per_device(acts, cotangent, momentum, params, band_index):
    any_ = pl.BlockSpec(memory_space=pl.ANY)
    dma = pltpu.SemaphoreType.DMA
    mixed, own, decoded = pl.pallas_call(
        kernel,
        out_shape=[jax.ShapeDtypeStruct((ROWS, KVW), F32)] * 3,
        in_specs=[any_] * 4,
        out_specs=[pl.BlockSpec(memory_space=pltpu.VMEM)] * 3,
        scratch_shapes=[
            pltpu.VMEM((16, 2 * TOK, 2 * ROWS), BF16),
            pltpu.VMEM((2 * TOK, KVW), BF16),
            pltpu.VMEM((KVW, 2 * TOK), BF16),
            pltpu.VMEM((16, KVW, 2 * ROWS), F32),
            pltpu.VMEM((N_MSG, HALF, 128), jnp.int16), pltpu.VMEM((N_MSG, HALF, 128), jnp.int16),
            pltpu.VMEM((N_MSG, 1, 128), F32), pltpu.VMEM((N_MSG, 1, 128), F32),
            pltpu.VMEM((4, HALF, 128), F32),
            pltpu.VMEM((8, 128, 256), BF16), pltpu.VMEM((8, 128, 256), BF16),
            pltpu.VMEM((8, 64, 256), F32),
            pltpu.VMEM((2, 8, 128), jnp.int32),
            pltpu.VMEM((ROWS, KVW), F32),
            pltpu.VMEM((8, 256), F32), pltpu.VMEM((3, 8, 256), F32),
            dma((3,)), dma, dma((16,)), dma, dma((2,)), dma((3,)),
            dma, dma((N_GROUP,)), dma, dma((N_GROUP,)), dma, dma,
            pltpu.SemaphoreType.REGULAR, pltpu.SemaphoreType.REGULAR,
        ],
        compiler_params=pltpu.CompilerParams(collective_id=0, has_side_effects=True, vmem_limit_bytes=53 * 2**20),
        name="step",
    )(acts, cotangent, momentum, band_index)
    update = decoded * lax.rsqrt(decoded * decoded + soft_width * soft_width)
    return (mixed - own)[None], params - step_rate * update


def solution(mesh):
    return jax.shard_map(
        per_device,
        mesh=mesh,
        in_specs=(
            P(("rep", "fsdp"), None),
            P(("rep", "fsdp"), None),
            P("rep", "fsdp", None),
            P("fsdp", None),
            P("fsdp", None, None),
        ),
        out_specs=(P("rep", "fsdp", None), P("fsdp", None)),
        check_vma=False,
    )
```

```python
import functools

import jax
import jax.numpy as jnp
import numpy as np
from jax import lax
from jax.experimental import pallas as pl
from jax.experimental.pallas import tpu as pltpu
from jax.sharding import PartitionSpec as P

MESH = pl.DeviceIdType.MESH
CH = 64
BAND = 128
ROWS = 128
KVW = 512
TOK = 768
HALF = KVW // 2
TOP = 32000.0
A1, B1, A2, B2, Z = 0, 32, 64, 72, 80
N_MSG = 82
N_GROUP = 38
beta_decay = 0.9
step_rate = 0.1
soft_width = 0.05
F32 = jnp.float32
BF16 = jnp.bfloat16


def basis_t():
    i = lax.broadcasted_iota(jnp.int32, (CH, CH), 0)
    k = lax.broadcasted_iota(jnp.int32, (CH, CH), 1)
    turn = jnp.bitwise_and((2 * i + 1) * k, 4 * CH - 1).astype(F32)
    return jnp.where(k == 0, (1.0 / CH) ** 0.5, (2.0 / CH) ** 0.5) * jnp.cos(turn * (np.pi / (2 * CH)))


def pack(out, scales, slot, val):
    scale = jnp.maximum(jnp.max(jnp.abs(val), axis=0, keepdims=True), 1e-30) * (1.0 / TOP)
    out[slot] = jnp.round(val * (1.0 / scale)).astype(jnp.int32).astype(jnp.int16)
    scales[slot] = scale


def unpack(buf, scales, slot):
    return buf[slot].astype(jnp.int32).astype(F32) * scales[slot]


def split(x):
    hi = x.astype(BF16)
    lo = (x - hi.astype(F32)).astype(BF16)
    return hi, lo


def kernel(acts, cot, mom, band, mixed, own, out,
           abuf, craw, ct, part, sbuf, rbuf, sscale, rscale,
           acc, w_hi, w_lo, ksel, idx, momv, vsum, vrecv,
           loc, dd_s, dd_r, co_s, co_r, misc, sem_s, sem_r, sem_ss, sem_rs, sem_sv, sem_rv, ready_z, ready_rep):
    f = lax.axis_index("fsdp")
    rep = lax.axis_index("rep")
    x, zh = lax.div(f, 16), lax.rem(lax.div(f, 8), 2)
    y, c = lax.rem(lax.div(f, 2), 4), lax.rem(f, 2)

    def fid(xx, zz, yy, cc):
        return ((xx * 2 + zz) * 4 + yy) * 2 + cc

    def px(d):
        return fid(lax.rem(x + d, 4), zh, y, c)

    def py(d):
        return fid(x, zh, lax.rem(y + d, 4), c)

    pz = fid(x, 1 - zh, y, c)
    pc = fid(x, zh, y, 1 - c)

    def remote(src, dst, s, r, dev):
        return pltpu.make_async_remote_copy(src, dst, s, r, device_id={"fsdp": dev}, device_id_type=MESH)

    def column(p, h, core):
        w, s, i = lax.div(p, 8), lax.rem(lax.div(p, 4), 2), lax.rem(p, 4)
        dx = lax.rem(6 - i - lax.div(i, 2) * (1 - 2 * lax.rem(i, 2)), 4)
        dy = 2 - h + s * (1 - 2 * h)
        zd = lax.rem(zh + 3 - w, 2)
        return pl.multiple_of(fid(lax.rem(x + dx, 4), zd, lax.rem(y + dy, 4), core) * ROWS, ROWS)

    def own_copy(p, h, sem):
        return pltpu.make_async_copy(acts.at[:, pl.ds(column(p, h, c), ROWS)],
                                     abuf.at[p, pl.ds(0, TOK), pl.ds(h * ROWS, ROWS)], loc.at[sem])

    def core_copy(p, h):
        return remote(acts.at[:, pl.ds(column(p, h, 1 - c), ROWS)],
                      abuf.at[p, pl.ds(TOK, TOK), pl.ds(h * ROWS, ROWS)], dd_s, dd_r.at[p], pc)

    cot_in = pltpu.make_async_copy(cot, craw.at[pl.ds(0, TOK)], misc.at[0])
    band_in = pltpu.make_async_copy(band, idx, misc.at[1])
    mom_in = pltpu.make_async_copy(mom.at[0], momv, misc.at[2])
    cot_over = [remote(cot.at[:, pl.ds(HALF * n, HALF)], craw.at[pl.ds(TOK, TOK), pl.ds(HALF * n, HALF)],
                       co_s, co_r.at[n], pc) for n in range(2)]

    barrier = pltpu.get_barrier_semaphore()
    for dev in (pc, px(1), px(2), px(3), py(1), py(2), py(3)):
        pl.semaphore_signal(barrier, inc=1, device_id={"fsdp": dev}, device_id_type=MESH)

    @pl.when(zh == 0)
    def _():
        pl.semaphore_signal(barrier, inc=1, device_id={"fsdp": pz}, device_id_type=MESH)

    for d in (1, 2, 3):
        @pl.when(rep + d < 4)
        def _():
            pl.semaphore_signal(barrier, inc=1, device_id={"rep": lax.rem(rep + d, 4)}, device_id_type=MESH)

    cot_in.start()
    own_copy(0, 0, 0).start()
    own_copy(0, 1, 0).start()
    pl.semaphore_wait(barrier, 7 + zh + rep)
    cot_over[0].start()
    core_copy(0, 0).start()
    core_copy(0, 1).start()
    cot_over[1].start()
    band_in.start()
    mom_in.start()

    @pl.when(zh == 1)
    def _():
        pl.semaphore_signal(ready_z, inc=1, device_id={"fsdp": pz}, device_id_type=MESH)

    for d in (1, 2, 3):
        @pl.when(rep >= d)
        def _():
            pl.semaphore_signal(ready_rep, inc=1, device_id={"rep": lax.rem(rep + 4 - d, 4)}, device_id_type=MESH)

    for sem, (a, b) in enumerate(((1, 6), (6, 16))):
        @pl.loop(a, b)
        def _(p):
            for h in range(2):
                core_copy(p, h).start()
                own_copy(p, h, sem + 1).start()

    cot_in.wait()
    ct[:, 0:TOK] = craw[0:TOK, :].T
    band_in.wait()

    b_hi, b_lo = split(basis_t())
    b2 = jnp.concatenate([b_hi, b_lo], axis=0)
    rowid = lax.broadcasted_iota(jnp.int32, (CH, BAND), 0)

    @pl.loop(0, 8)
    def _(g):
        b, jp = lax.div(g, 4), lax.rem(g, 4)
        w_hi[g] = jnp.zeros((128, 256), BF16)
        w_lo[g] = jnp.zeros((128, 256), BF16)
        for t in range(2):
            at = idx[b, pl.ds(2 * jp + t, 1), :]
            k1 = jnp.where(rowid == jnp.right_shift(at, 6), 1.0, 0.0).astype(BF16)
            l1 = jnp.where(rowid == jnp.bitwise_and(at, 63), 1.0, 0.0).astype(BF16)
            sel = jnp.dot(b2, jnp.concatenate([k1, l1], axis=1), preferred_element_type=F32)
            ksel[g, :, 128 * t:128 * t + 128] = sel[0:64, 0:128] + sel[64:128, 0:128]
            w_hi[g, 64 * t:64 * t + 64, 128 * t:128 * t + 128] = sel[0:64, 128:256].astype(BF16)
            w_lo[g, 64 * t:64 * t + 64, 128 * t:128 * t + 128] = sel[64:128, 128:256].astype(BF16)

    def take(group, *slots):
        n = pl.ds(0, len(slots))
        remote(rbuf.at[n], rbuf.at[n], sem_s, sem_r.at[group], pz).wait_recv()
        remote(rscale.at[n], rscale.at[n], sem_ss, sem_rs.at[group], pz).wait_recv()
        return sum(unpack(rbuf, rscale, slot) for slot in slots)

    def send(slot, group, dev, val):
        pack(sbuf, sscale, slot, val)
        remote(sbuf.at[slot], rbuf.at[slot], sem_s, sem_r.at[group], dev).start()
        remote(sscale.at[slot], rscale.at[slot], sem_ss, sem_rs.at[group], dev).start()

    def send_a1(slot, d, val):
        p, h = lax.div(slot, 2), lax.rem(slot, 2)
        send(A1 + slot, 2 * lax.div(p, 4) + h + 8 * lax.div(lax.rem(p, 4) + 3, 4), px(d), val)

    def send_b1(slot, d, val):
        p, h = lax.div(slot, 2), lax.rem(slot, 2)
        w, s, i = lax.div(p, 8), lax.rem(lax.div(p, 4), 2), lax.rem(p, 4)
        send(B1 + slot, 24 + 4 * w + i - 8 * (1 - s) * (1 - h), py(d), val)

    def send_2(n, w, q, val):
        to = (py, px)[n](2 - q + 3 * lax.div(q, 2))
        send((A2, B2)[n] + 4 * w + q, 32 + 2 * n + w, to, val)

    def half(which, slot):
        p, h = lax.div(slot, 2), lax.rem(slot, 2)
        return part[p, pl.ds(which * HALF, HALF), pl.ds(pl.multiple_of(h * ROWS, ROWS), ROWS)]

    def send_a(p):
        i = lax.rem(p, 4)
        for h in range(2):
            go, d = (lax.rem(i, 2) == 0, 1 + i) if h == 0 else (i + 2 * lax.div(p, 12) < 2, 3 - 2 * i)

            @pl.when(go)
            def _():
                send_a1(2 * p + h, d, part[p, 0:HALF, h * ROWS:(h + 1) * ROWS])

    def send_b(p):
        s, odd = lax.rem(lax.div(p, 4), 2), lax.rem(p, 2)
        last = lax.div(p, 11) - lax.div(p, 12)
        for h in range(2):
            go, d = (s * odd + last == 0, 1 + 2 * odd + 2 * s) if h == 0 else ((1 - s) * odd - last == 1, 1)

            @pl.when(go)
            def _():
                send_b1(2 * p + h, d, part[p, HALF:KVW, h * ROWS:(h + 1) * ROWS])

    def loaded(a, b, sem):
        there = abuf.at[pl.ds(a, b - a), pl.ds(0, TOK)]
        pltpu.make_async_copy(there, there, loc.at[sem]).wait()

    def arrive(p):
        there = abuf.at[p, pl.ds(TOK, TOK)]
        remote(there, there, dd_s, dd_r.at[p], pc).wait_recv()

    def produce(a, b):
        @pl.loop(a, b)
        def _(p):
            arrive(p)
            part[p] = jnp.dot(ct[...], abuf[p], preferred_element_type=F32)
            send_a(p)
            send_b(p)

    def late():
        send_a1(25, 3, part[12, 0:HALF, ROWS:2 * ROWS])
        send_b1(22, 3, part[11, HALF:KVW, 0:ROWS])
        send_a1(27, 1, part[13, 0:HALF, ROWS:2 * ROWS])
        send_b1(23, 1, part[11, HALF:KVW, ROWS:2 * ROWS])

    def relay_a(w, s, a=0, b=2):
        @pl.loop(a, b)
        def _(h):
            got = 16 * w + 8 * s + h
            slot = got + 2 + 2 * h
            send_a1(slot, 1 + 2 * h, take(4 * w + 2 * s + h, A1 + got) + half(0, slot))

    def relay_b(w, a, b):
        @pl.loop(a, b)
        def _(i):
            odd = lax.rem(i, 2)
            got = 16 * w + 2 * i
            slot = got + 1 + 7 * odd
            send_b1(slot, 1 + 2 * odd, take(16 + 4 * w + i, B1 + got) + half(1, slot))

    def first_sum(w, a, b):
        @pl.loop(a, b)
        def _(q):
            base = 16 * w + 8 * lax.div(q, 2) + lax.rem(q, 2)
            total = half(0, base + 6) + take(8 + 4 * w + q, A1 + base + 2, A1 + base + 4)

            @pl.when(q == 3)
            def _():
                acc[2 * w] = total

            @pl.when(q != 3)
            def _():
                send_2(0, w, q, total)

            got = 16 * w + 2 * q
            total_b = half(1, got + 9) + take(24 + 4 * w + q, B1 + got + 1, B1 + got + 8)

            @pl.when(q == 3)
            def _():
                acc[2 * w + 1] = total_b

            @pl.when(q != 3)
            def _():
                send_2(1, w, q, total_b)

    def second_sum(w, n):
        at = (A2, B2)[n] + 4 * w
        return acc[2 * w + n] + take(32 + 2 * n + w, at, at + 1, at + 2)

    loaded(0, 1, 0)
    arrive(0)
    for n in range(2):
        cot_over[n].wait_recv()
        ct[HALF * n:HALF * n + HALF, TOK:2 * TOK] = craw[TOK:2 * TOK, HALF * n:HALF * n + HALF].T
        part[0, HALF * n:HALF * n + HALF, :] = jnp.dot(ct[HALF * n:HALF * n + HALF, :], abuf[0],
                                                       preferred_element_type=F32)
        (send_a, send_b)[n](jnp.int32(0))
    loaded(1, 6, 1)
    produce(1, 5)
    relay_a(0, 0)
    relay_b(0, 0, 1)
    loaded(6, 16, 2)
    produce(5, 7)
    relay_b(0, 1, 3)
    produce(7, 9)
    relay_b(0, 3, 4)
    relay_a(0, 1)
    produce(9, 14)
    first_sum(0, 0, 4)
    produce(14, 16)
    late()
    relay_a(1, 0)
    relay_b(1, 0, 3)
    relay_a(1, 1, 0, 1)
    @pl.when(zh == 0)
    def _():
        pl.semaphore_wait(ready_z, 1)

    for n in range(2):
        send(Z + n, 36 + n, pz, second_sum(0, n))
    relay_a(1, 1, 1, 2)
    relay_b(1, 3, 4)
    first_sum(1, 0, 4)
    def group(g):
        b, jp = g // 4, g % 4
        return slice(64 * b, 64 * b + 64), slice(128 * jp, 128 * jp + 128)

    mom_in.wait()
    for n in range(2):
        total = second_sum(1, n) + take(36 + n, Z + n)
        cols = slice(HALF * n, HALF * n + HALF)
        mixed[:, cols] = beta_decay * momv[:, cols] + total.T
        for g in (2 * n, 2 * n + 1, 2 * n + 4, 2 * n + 5):
            rows, lanes = group(g)
            hi, lo = split(mixed[rows, lanes])
            q = (jnp.dot(hi, w_hi[g], preferred_element_type=F32) + jnp.dot(lo, w_hi[g], preferred_element_type=F32)
                 + jnp.dot(hi, w_lo[g], preferred_element_type=F32))
            vsum[g:g + 1, :] = jnp.sum(q * ksel[g], axis=0, keepdims=True)

    @pl.when(rep < 3)
    def _():
        pl.semaphore_wait(ready_rep, 3 - rep)

    swap = [pltpu.make_async_remote_copy(vsum, vrecv.at[d - 1], sem_sv, sem_rv,
                                         device_id={"rep": lax.rem(rep + d, 4)}, device_id_type=MESH)
            for d in (1, 2, 3)]
    for cp in swap:
        cp.start()
    swapped = pltpu.make_async_remote_copy(vrecv, vrecv, sem_sv, sem_rv,
                                           device_id={"rep": lax.rem(rep + 1, 4)}, device_id_type=MESH)

    def nt(a, b):
        return lax.dot_general(a, b, (((1,), (1,)), ((), ())), preferred_element_type=F32)

    def decode(values, g):
        hi, lo = split(ksel[g] * values)
        return nt(hi, w_hi[g]) + nt(lo, w_hi[g]) + nt(hi, w_lo[g])

    for g in range(8):
        rows, cols = group(g)
        own[rows, cols] = decode(vsum[g:g + 1, :], g)

    swapped.wait_recv()
    shared = (vsum[...] + vrecv[0] + vrecv[1] + vrecv[2]) * 0.25
    for g in range(8):
        rows, cols = group(g)
        out[rows, cols] = decode(shared[g:g + 1, :], g)

    n = pl.ds(0, 62)
    remote(sbuf.at[n], rbuf.at[n], sem_s, sem_r.at[0], pz).wait_send()
    remote(sscale.at[n], rscale.at[n], sem_ss, sem_rs.at[0], pz).wait_send()
    there = abuf.at[:, pl.ds(0, TOK)]
    remote(there, there, dd_s, dd_r.at[0], pc).wait_send()
    there = craw.at[pl.ds(0, TOK)]
    remote(there, there, co_s, co_r.at[0], pc).wait_send()
    swapped.wait_send()


def per_device(acts, cotangent, momentum, params, band_index):
    any_ = pl.BlockSpec(memory_space=pl.ANY)
    dma = pltpu.SemaphoreType.DMA
    mixed, own, decoded = pl.pallas_call(
        kernel,
        out_shape=[jax.ShapeDtypeStruct((ROWS, KVW), F32)] * 3,
        in_specs=[any_] * 4,
        out_specs=[pl.BlockSpec(memory_space=pltpu.VMEM)] * 3,
        scratch_shapes=[
            pltpu.VMEM((16, 2 * TOK, 2 * ROWS), BF16),
            pltpu.VMEM((2 * TOK, KVW), BF16),
            pltpu.VMEM((KVW, 2 * TOK), BF16),
            pltpu.VMEM((16, KVW, 2 * ROWS), F32),
            pltpu.VMEM((N_MSG, HALF, 128), jnp.int16), pltpu.VMEM((N_MSG, HALF, 128), jnp.int16),
            pltpu.VMEM((N_MSG, 1, 128), F32), pltpu.VMEM((N_MSG, 1, 128), F32),
            pltpu.VMEM((4, HALF, 128), F32),
            pltpu.VMEM((8, 128, 256), BF16), pltpu.VMEM((8, 128, 256), BF16),
            pltpu.VMEM((8, 64, 256), F32),
            pltpu.VMEM((2, 8, 128), jnp.int32),
            pltpu.VMEM((ROWS, KVW), F32),
            pltpu.VMEM((8, 256), F32), pltpu.VMEM((3, 8, 256), F32),
            dma((3,)), dma, dma((16,)), dma, dma((2,)), dma((3,)),
            dma, dma((N_GROUP,)), dma, dma((N_GROUP,)), dma, dma,
            pltpu.SemaphoreType.REGULAR, pltpu.SemaphoreType.REGULAR,
        ],
        compiler_params=pltpu.CompilerParams(collective_id=0, has_side_effects=True, vmem_limit_bytes=53 * 2**20),
        name="step",
    )(acts, cotangent, momentum, pltpu.with_memory_space_constraint(band_index, pltpu.HBM))
    update = decoded * lax.rsqrt(decoded * decoded + soft_width * soft_width)
    return (mixed - own)[None], params - step_rate * update


def solution(mesh):
    return jax.shard_map(
        per_device,
        mesh=mesh,
        in_specs=(
            P(("rep", "fsdp"), None),
            P(("rep", "fsdp"), None),
            P("rep", "fsdp", None),
            P("fsdp", None),
            P("fsdp", None, None),
        ),
        out_specs=(P("rep", "fsdp", None), P("fsdp", None)),
        check_vma=False,
    )
```

```python
import functools

import jax
import jax.numpy as jnp
import numpy as np
from jax import lax
from jax.experimental import pallas as pl
from jax.experimental.pallas import tpu as pltpu
from jax.sharding import PartitionSpec as P

MESH = pl.DeviceIdType.MESH
CH = 64
BAND = 128
ROWS = 128
KVW = 512
TOK = 768
HALF = KVW // 2
TOP = 32000.0
A1, B1, A2, B2, Z = 0, 32, 64, 72, 80
N_MSG = 82
N_GROUP = 38
beta_decay = 0.9
step_rate = 0.1
soft_width = 0.05
F32 = jnp.float32
BF16 = jnp.bfloat16


def basis_t():
    i = lax.broadcasted_iota(jnp.int32, (CH, CH), 0)
    k = lax.broadcasted_iota(jnp.int32, (CH, CH), 1)
    turn = jnp.bitwise_and((2 * i + 1) * k, 4 * CH - 1).astype(F32)
    return jnp.where(k == 0, (1.0 / CH) ** 0.5, (2.0 / CH) ** 0.5) * jnp.cos(turn * (np.pi / (2 * CH)))


def pack(out, scales, slot, val):
    scale = jnp.maximum(jnp.max(jnp.abs(val), axis=0, keepdims=True), 1e-30) * (1.0 / TOP)
    out[slot] = jnp.round(val * (1.0 / scale)).astype(jnp.int32).astype(jnp.int16)
    scales[slot] = scale


def unpack(buf, scales, slot):
    return buf[slot].astype(jnp.int32).astype(F32) * scales[slot]


def split(x):
    hi = x.astype(BF16)
    lo = (x - hi.astype(F32)).astype(BF16)
    return hi, lo


def kernel(acts, cot, mom, band, mixed, own, out,
           abuf, craw, ct, part, sbuf, rbuf, sscale, rscale,
           acc, w_hi, w_lo, ksel, idx, momv, vsum, vrecv,
           loc, dd_s, dd_r, co_s, co_r, misc, sem_s, sem_r, sem_ss, sem_rs, sem_sv, sem_rv, ready_x, ready_y, ready_z, ready_rep):
    f = lax.axis_index("fsdp")
    rep = lax.axis_index("rep")
    x, zh = lax.div(f, 16), lax.rem(lax.div(f, 8), 2)
    y, c = lax.rem(lax.div(f, 2), 4), lax.rem(f, 2)

    def fid(xx, zz, yy, cc):
        return ((xx * 2 + zz) * 4 + yy) * 2 + cc

    def px(d):
        return fid(lax.rem(x + d, 4), zh, y, c)

    def py(d):
        return fid(x, zh, lax.rem(y + d, 4), c)

    pz = fid(x, 1 - zh, y, c)
    pc = fid(x, zh, y, 1 - c)

    def remote(src, dst, s, r, dev):
        return pltpu.make_async_remote_copy(src, dst, s, r, device_id={"fsdp": dev}, device_id_type=MESH)

    def column(p, h, core):
        w, s, i = lax.div(p, 8), lax.rem(lax.div(p, 4), 2), lax.rem(p, 4)
        dx = lax.rem(6 - i - lax.div(i, 2) * (1 - 2 * lax.rem(i, 2)), 4)
        dy = 2 - h + s * (1 - 2 * h)
        zd = lax.rem(zh + 3 - w, 2)
        return pl.multiple_of(fid(lax.rem(x + dx, 4), zd, lax.rem(y + dy, 4), core) * ROWS, ROWS)

    def own_copy(p, h, sem):
        return pltpu.make_async_copy(acts.at[:, pl.ds(column(p, h, c), ROWS)],
                                     abuf.at[p, pl.ds(0, TOK), pl.ds(h * ROWS, ROWS)], loc.at[sem])

    def core_copy(p, h):
        return remote(acts.at[:, pl.ds(column(p, h, 1 - c), ROWS)],
                      abuf.at[p, pl.ds(TOK, TOK), pl.ds(h * ROWS, ROWS)], dd_s, dd_r.at[p], pc)

    cot_in = pltpu.make_async_copy(cot, craw.at[pl.ds(0, TOK)], misc.at[0])
    band_in = pltpu.make_async_copy(band, idx, misc.at[1])
    mom_in = pltpu.make_async_copy(mom.at[0], momv, misc.at[2])
    cot_over = [remote(cot.at[:, pl.ds(HALF * n, HALF)], craw.at[pl.ds(TOK, TOK), pl.ds(HALF * n, HALF)],
                       co_s, co_r.at[n], pc) for n in range(2)]

    barrier = pltpu.get_barrier_semaphore()
    for dev in (pc, px(1), px(3), py(1), py(3)):
        pl.semaphore_signal(barrier, inc=1, device_id={"fsdp": dev}, device_id_type=MESH)

    @pl.when(x < 2)
    def _():
        pl.semaphore_signal(barrier, inc=1, device_id={"fsdp": px(2)}, device_id_type=MESH)

    @pl.when(y < 2)
    def _():
        pl.semaphore_signal(barrier, inc=1, device_id={"fsdp": py(2)}, device_id_type=MESH)

    @pl.when(zh == 0)
    def _():
        pl.semaphore_signal(barrier, inc=1, device_id={"fsdp": pz}, device_id_type=MESH)

    for d in (1, 2, 3):
        @pl.when(rep + d < 4)
        def _():
            pl.semaphore_signal(barrier, inc=1, device_id={"rep": lax.rem(rep + d, 4)}, device_id_type=MESH)

    cot_in.start()
    own_copy(0, 0, 0).start()
    own_copy(0, 1, 0).start()
    pl.semaphore_wait(barrier, 5 + lax.div(x, 2) + lax.div(y, 2) + zh + rep)
    cot_over[0].start()
    core_copy(0, 0).start()
    core_copy(0, 1).start()
    cot_over[1].start()
    band_in.start()
    mom_in.start()

    @pl.when(x >= 2)
    def _():
        pl.semaphore_signal(ready_x, inc=1, device_id={"fsdp": px(2)}, device_id_type=MESH)

    @pl.when(y >= 2)
    def _():
        pl.semaphore_signal(ready_y, inc=1, device_id={"fsdp": py(2)}, device_id_type=MESH)

    @pl.when(zh == 1)
    def _():
        pl.semaphore_signal(ready_z, inc=1, device_id={"fsdp": pz}, device_id_type=MESH)

    for d in (1, 2, 3):
        @pl.when(rep >= d)
        def _():
            pl.semaphore_signal(ready_rep, inc=1, device_id={"rep": lax.rem(rep + 4 - d, 4)}, device_id_type=MESH)

    for sem, (a, b) in enumerate(((1, 6), (6, 16))):
        @pl.loop(a, b)
        def _(p):
            for h in range(2):
                core_copy(p, h).start()
                own_copy(p, h, sem + 1).start()

    cot_in.wait()
    ct[:, 0:TOK] = craw[0:TOK, :].T
    band_in.wait()

    b_hi, b_lo = split(basis_t())
    b2 = jnp.concatenate([b_hi, b_lo], axis=0)
    rowid = lax.broadcasted_iota(jnp.int32, (CH, BAND), 0)

    @pl.loop(0, 8)
    def _(g):
        b, jp = lax.div(g, 4), lax.rem(g, 4)
        w_hi[g] = jnp.zeros((128, 256), BF16)
        w_lo[g] = jnp.zeros((128, 256), BF16)
        for t in range(2):
            at = idx[b, pl.ds(2 * jp + t, 1), :]
            k1 = jnp.where(rowid == jnp.right_shift(at, 6), 1.0, 0.0).astype(BF16)
            l1 = jnp.where(rowid == jnp.bitwise_and(at, 63), 1.0, 0.0).astype(BF16)
            sel = jnp.dot(b2, jnp.concatenate([k1, l1], axis=1), preferred_element_type=F32)
            ksel[g, :, 128 * t:128 * t + 128] = sel[0:64, 0:128] + sel[64:128, 0:128]
            w_hi[g, 64 * t:64 * t + 64, 128 * t:128 * t + 128] = sel[0:64, 128:256].astype(BF16)
            w_lo[g, 64 * t:64 * t + 64, 128 * t:128 * t + 128] = sel[64:128, 128:256].astype(BF16)

    def take(group, *slots):
        n = pl.ds(0, len(slots))
        remote(rbuf.at[n], rbuf.at[n], sem_s, sem_r.at[group], pz).wait_recv()
        remote(rscale.at[n], rscale.at[n], sem_ss, sem_rs.at[group], pz).wait_recv()
        return sum(unpack(rbuf, rscale, slot) for slot in slots)

    def send(slot, group, dev, val):
        pack(sbuf, sscale, slot, val)
        remote(sbuf.at[slot], rbuf.at[slot], sem_s, sem_r.at[group], dev).start()
        remote(sscale.at[slot], rscale.at[slot], sem_ss, sem_rs.at[group], dev).start()

    def send_a1(slot, d, val):
        p, h = lax.div(slot, 2), lax.rem(slot, 2)
        send(A1 + slot, 2 * lax.div(p, 4) + h + 8 * lax.div(lax.rem(p, 4) + 3, 4), px(d), val)

    def send_b1(slot, d, val):
        p, h = lax.div(slot, 2), lax.rem(slot, 2)
        w, s, i = lax.div(p, 8), lax.rem(lax.div(p, 4), 2), lax.rem(p, 4)
        send(B1 + slot, 24 + 4 * w + i - 8 * (1 - s) * (1 - h), py(d), val)

    def send_2(n, w, q, val):
        to = (py, px)[n](2 - q + 3 * lax.div(q, 2))
        send((A2, B2)[n] + 4 * w + q, 32 + 2 * n + w, to, val)

    def half(which, slot):
        p, h = lax.div(slot, 2), lax.rem(slot, 2)
        return part[p, pl.ds(which * HALF, HALF), pl.ds(pl.multiple_of(h * ROWS, ROWS), ROWS)]

    def send_a(p):
        i = lax.rem(p, 4)
        for h in range(2):
            go, d = (lax.rem(i, 2) == 0, 1 + i) if h == 0 else (i + 2 * lax.div(p, 12) < 2, 3 - 2 * i)

            @pl.when(go)
            def _():
                send_a1(2 * p + h, d, part[p, 0:HALF, h * ROWS:(h + 1) * ROWS])

    def send_b(p):
        s, odd = lax.rem(lax.div(p, 4), 2), lax.rem(p, 2)
        last = lax.div(p, 11) - lax.div(p, 12)
        for h in range(2):
            go, d = (s * odd + last == 0, 1 + 2 * odd + 2 * s) if h == 0 else ((1 - s) * odd - last == 1, 1)

            @pl.when(go)
            def _():
                send_b1(2 * p + h, d, part[p, HALF:KVW, h * ROWS:(h + 1) * ROWS])

    def loaded(a, b, sem):
        there = abuf.at[pl.ds(a, b - a), pl.ds(0, TOK)]
        pltpu.make_async_copy(there, there, loc.at[sem]).wait()

    def arrive(p):
        there = abuf.at[p, pl.ds(TOK, TOK)]
        remote(there, there, dd_s, dd_r.at[p], pc).wait_recv()

    def produce(a, b):
        @pl.loop(a, b)
        def _(p):
            arrive(p)
            part[p] = jnp.dot(ct[...], abuf[p], preferred_element_type=F32)
            send_a(p)
            send_b(p)

    def late():
        send_a1(25, 3, part[12, 0:HALF, ROWS:2 * ROWS])
        send_b1(22, 3, part[11, HALF:KVW, 0:ROWS])
        send_a1(27, 1, part[13, 0:HALF, ROWS:2 * ROWS])
        send_b1(23, 1, part[11, HALF:KVW, ROWS:2 * ROWS])

    def relay_a(w, s, a=0, b=2):
        @pl.loop(a, b)
        def _(h):
            got = 16 * w + 8 * s + h
            slot = got + 2 + 2 * h
            send_a1(slot, 1 + 2 * h, take(4 * w + 2 * s + h, A1 + got) + half(0, slot))

    def relay_b(w, a, b):
        @pl.loop(a, b)
        def _(i):
            odd = lax.rem(i, 2)
            got = 16 * w + 2 * i
            slot = got + 1 + 7 * odd
            send_b1(slot, 1 + 2 * odd, take(16 + 4 * w + i, B1 + got) + half(1, slot))

    def first_sum(w, a, b):
        @pl.loop(a, b)
        def _(q):
            base = 16 * w + 8 * lax.div(q, 2) + lax.rem(q, 2)
            total = half(0, base + 6) + take(8 + 4 * w + q, A1 + base + 2, A1 + base + 4)

            @pl.when(q == 3)
            def _():
                acc[2 * w] = total

            @pl.when(q != 3)
            def _():
                send_2(0, w, q, total)

            got = 16 * w + 2 * q
            total_b = half(1, got + 9) + take(24 + 4 * w + q, B1 + got + 1, B1 + got + 8)

            @pl.when(q == 3)
            def _():
                acc[2 * w + 1] = total_b

            @pl.when(q != 3)
            def _():
                send_2(1, w, q, total_b)

    def second_sum(w, n):
        at = (A2, B2)[n] + 4 * w
        return acc[2 * w + n] + take(32 + 2 * n + w, at, at + 1, at + 2)

    loaded(0, 1, 0)
    arrive(0)
    for n in range(2):
        cot_over[n].wait_recv()
        ct[HALF * n:HALF * n + HALF, TOK:2 * TOK] = craw[TOK:2 * TOK, HALF * n:HALF * n + HALF].T
        part[0, HALF * n:HALF * n + HALF, :] = jnp.dot(ct[HALF * n:HALF * n + HALF, :], abuf[0],
                                                       preferred_element_type=F32)
        (send_a, send_b)[n](jnp.int32(0))
    loaded(1, 6, 1)
    produce(1, 5)
    relay_a(0, 0)
    relay_b(0, 0, 1)
    loaded(6, 16, 2)
    produce(5, 7)
    relay_b(0, 1, 3)
    produce(7, 9)
    relay_b(0, 3, 4)
    relay_a(0, 1)
    produce(9, 14)

    @pl.when(x < 2)
    def _():
        pl.semaphore_wait(ready_x, 1)

    @pl.when(y < 2)
    def _():
        pl.semaphore_wait(ready_y, 1)

    first_sum(0, 0, 4)
    produce(14, 16)
    late()
    relay_a(1, 0)
    relay_b(1, 0, 3)
    relay_a(1, 1, 0, 1)
    @pl.when(zh == 0)
    def _():
        pl.semaphore_wait(ready_z, 1)

    for n in range(2):
        send(Z + n, 36 + n, pz, second_sum(0, n))
    relay_a(1, 1, 1, 2)
    relay_b(1, 3, 4)
    first_sum(1, 0, 4)
    def group(g):
        b, jp = g // 4, g % 4
        return slice(64 * b, 64 * b + 64), slice(128 * jp, 128 * jp + 128)

    mom_in.wait()
    for n in range(2):
        total = second_sum(1, n) + take(36 + n, Z + n)
        cols = slice(HALF * n, HALF * n + HALF)
        mixed[:, cols] = beta_decay * momv[:, cols] + total.T
        for g in (2 * n, 2 * n + 1, 2 * n + 4, 2 * n + 5):
            rows, lanes = group(g)
            hi, lo = split(mixed[rows, lanes])
            q = (jnp.dot(hi, w_hi[g], preferred_element_type=F32) + jnp.dot(lo, w_hi[g], preferred_element_type=F32)
                 + jnp.dot(hi, w_lo[g], preferred_element_type=F32))
            vsum[g:g + 1, :] = jnp.sum(q * ksel[g], axis=0, keepdims=True)

    @pl.when(rep < 3)
    def _():
        pl.semaphore_wait(ready_rep, 3 - rep)

    swap = [pltpu.make_async_remote_copy(vsum, vrecv.at[d - 1], sem_sv, sem_rv,
                                         device_id={"rep": lax.rem(rep + d, 4)}, device_id_type=MESH)
            for d in (1, 2, 3)]
    for cp in swap:
        cp.start()
    swapped = pltpu.make_async_remote_copy(vrecv, vrecv, sem_sv, sem_rv,
                                           device_id={"rep": lax.rem(rep + 1, 4)}, device_id_type=MESH)

    def nt(a, b):
        return lax.dot_general(a, b, (((1,), (1,)), ((), ())), preferred_element_type=F32)

    def decode(values, g):
        hi, lo = split(ksel[g] * values)
        return nt(hi, w_hi[g]) + nt(lo, w_hi[g]) + nt(hi, w_lo[g])

    for g in range(8):
        rows, cols = group(g)
        own[rows, cols] = decode(vsum[g:g + 1, :], g)

    swapped.wait_recv()
    shared = (vsum[...] + vrecv[0] + vrecv[1] + vrecv[2]) * 0.25
    for g in range(8):
        rows, cols = group(g)
        out[rows, cols] = decode(shared[g:g + 1, :], g)

    n = pl.ds(0, 62)
    remote(sbuf.at[n], rbuf.at[n], sem_s, sem_r.at[0], pz).wait_send()
    remote(sscale.at[n], rscale.at[n], sem_ss, sem_rs.at[0], pz).wait_send()
    there = abuf.at[:, pl.ds(0, TOK)]
    remote(there, there, dd_s, dd_r.at[0], pc).wait_send()
    there = craw.at[pl.ds(0, TOK)]
    remote(there, there, co_s, co_r.at[0], pc).wait_send()
    swapped.wait_send()


def per_device(acts, cotangent, momentum, params, band_index):
    any_ = pl.BlockSpec(memory_space=pl.ANY)
    dma = pltpu.SemaphoreType.DMA
    mixed, own, decoded = pl.pallas_call(
        kernel,
        out_shape=[jax.ShapeDtypeStruct((ROWS, KVW), F32)] * 3,
        in_specs=[any_] * 4,
        out_specs=[pl.BlockSpec(memory_space=pltpu.VMEM)] * 3,
        scratch_shapes=[
            pltpu.VMEM((16, 2 * TOK, 2 * ROWS), BF16),
            pltpu.VMEM((2 * TOK, KVW), BF16),
            pltpu.VMEM((KVW, 2 * TOK), BF16),
            pltpu.VMEM((16, KVW, 2 * ROWS), F32),
            pltpu.VMEM((N_MSG, HALF, 128), jnp.int16), pltpu.VMEM((N_MSG, HALF, 128), jnp.int16),
            pltpu.VMEM((N_MSG, 1, 128), F32), pltpu.VMEM((N_MSG, 1, 128), F32),
            pltpu.VMEM((4, HALF, 128), F32),
            pltpu.VMEM((8, 128, 256), BF16), pltpu.VMEM((8, 128, 256), BF16),
            pltpu.VMEM((8, 64, 256), F32),
            pltpu.VMEM((2, 8, 128), jnp.int32),
            pltpu.VMEM((ROWS, KVW), F32),
            pltpu.VMEM((8, 256), F32), pltpu.VMEM((3, 8, 256), F32),
            dma((3,)), dma, dma((16,)), dma, dma((2,)), dma((3,)),
            dma, dma((N_GROUP,)), dma, dma((N_GROUP,)), dma, dma,
            pltpu.SemaphoreType.REGULAR, pltpu.SemaphoreType.REGULAR,
            pltpu.SemaphoreType.REGULAR, pltpu.SemaphoreType.REGULAR,
        ],
        compiler_params=pltpu.CompilerParams(collective_id=0, has_side_effects=True, vmem_limit_bytes=53 * 2**20),
        name="step",
    )(acts, cotangent, momentum, pltpu.with_memory_space_constraint(band_index, pltpu.HBM))
    update = decoded * lax.rsqrt(decoded * decoded + soft_width * soft_width)
    return (mixed - own)[None], params - step_rate * update


def solution(mesh):
    return jax.shard_map(
        per_device,
        mesh=mesh,
        in_specs=(
            P(("rep", "fsdp"), None),
            P(("rep", "fsdp"), None),
            P("rep", "fsdp", None),
            P("fsdp", None),
            P("fsdp", None, None),
        ),
        out_specs=(P("rep", "fsdp", None), P("fsdp", None)),
        check_vma=False,
    )
```
